32 devices in a mesh: groups: 2 (over x), lvl: 8 (over z, y), stu: 2 (over core).
Axes of the slice: x: 2, y: 2, z: 4, core: 2. Of those that a mesh axis runs over, the one named last changes fastest.
Arguments:
- student_factor: float32 [4096, 256], P(('groups', 'stu', 'lvl')), parts along dimension 0, may hold values from -1.5 to 1.5
- level_factor: float32 [16384, 256], P(('groups', 'lvl', 'stu')), parts along dimension 0, may hold values from -1.5 to 1.5
- block_position: int32 [4, 8, 24], P(('groups', 'stu'), 'lvl'), parts along dimension 0, may hold values from 0 to 63, as said below
- block_count: int32 [4, 8], P(('groups', 'stu'), 'lvl'), parts along dimension 0, may hold values from 1 to 24, as said below
- outcome: int32 [4, 8, 24, 128, 128], P(('groups', 'stu'), 'lvl'), parts along dimension 0, may hold values 0 or 1
Outputs:
- student_out: float32 [4096, 256], P(('groups', 'stu', 'lvl')), parts along dimension 0
- level_out: float32 [16384, 256], P(('groups', 'lvl', 'stu')), parts along dimension 0
The draws below stay inside these ranges and needn't reach their ends.
There are 2 independent parts, one for each index of `groups`. The reference program is written for one: setup_inputs(seed, part) draws one part's arguments, and reference() takes and returns one part's arrays. A program takes and returns all parts, laid end to end along the dimension named above; each array names one. Nothing has to cross between parts.
Inputs may be any that keep to these rules, and one draw needn't show every extreme that they name: `block_position`: within one tile the positions of all 24 slots are distinct, each names a block of the tile. `block_count`: counts are very uneven between tiles; some tile uses all its slots.
All inputs are finite; a program needn't handle non-finite values. No bound on the sum of `outcome` on one device may be relied on, other than what follows from the above.
Results may differ from the reference program's by a relative error of at most 0.008.
Values may be sent and summed in bfloat16 or wider, within the bound.
No kernel may reach another device: no remote copies, remote signals or barrier semaphores. Data moves between devices by JAX's collectives and lax.ppermute only.
A program may use at most 128 MiB of HBM per device.

```python
import jax
import jax.numpy as jnp
from jax import lax

R = 256
BLK = 128
ITERS = 2
STU_PANEL = 1024
LVL_PANEL = 1024
POSITIONS = 64
MAXB = 24
STUDENTS = 2048
LEVELS = 8192
N_LVL = 8
N_STU = 2


def draw_block_position(key, part):
    key = jax.random.fold_in(key, 7)
    tiles = N_STU * N_LVL
    keys = jax.random.split(key, tiles)
    orders = jax.vmap(lambda k: jax.random.permutation(k, POSITIONS)[:MAXB])(keys)
    return orders.reshape(N_STU, N_LVL, MAXB).astype(jnp.int32)


def draw_block_count(key, part):
    key = jax.random.fold_in(key, 11)
    first_key, second_key, third_key = jax.random.split(key, 3)
    tiles = N_STU * N_LVL
    first = jax.random.randint(first_key, (tiles,), 1, MAXB + 1)
    second = jax.random.randint(second_key, (tiles,), 1, MAXB + 1)
    lower = jnp.minimum(first, second)
    chosen = jax.random.randint(third_key, (), 0, tiles)
    filled = jnp.where(jnp.arange(tiles) == chosen, MAXB, lower)
    return filled.reshape(N_STU, N_LVL).astype(jnp.int32)


def set_ends(entries, stream_key, low, high):
    spot = [jax.random.randint(jax.random.fold_in(stream_key, axis), (), 0, length) for axis, length in enumerate(entries.shape)]
    longest = entries.shape.index(max(entries.shape))
    next_to = spot[:longest] + [(spot[longest] + 1) % entries.shape[longest]] + spot[longest + 1:]
    return entries.at[tuple(spot)].set(low).at[tuple(next_to)].set(high)


def level_of(key, extent, pieces, smallest, largest):
    def one(dim, blocks):
        steps = jax.random.uniform(jax.random.fold_in(jax.random.fold_in(key, 6), dim), (blocks,), jnp.float32, smallest / len(pieces), largest / len(pieces))
        return jnp.repeat(jnp.exp(steps), extent[dim] // blocks).reshape((-1,) + (1,) * (len(extent) - dim - 1))

    factor_of = one(*pieces[0])
    for cut in pieces[1:]:
        factor_of = factor_of * one(*cut)
    return factor_of


def centred(stream_key, extent, spread, bound, cuts=(), kind=jnp.bfloat16):
    drawn = jax.random.normal(stream_key, extent, jnp.float32) * spread
    if len(cuts) > 0:
        drawn = level_of(stream_key, extent, cuts, -0.22, 0.18) * drawn
    return jnp.clip(drawn, min=-bound, max=bound).astype(kind)


def setup_inputs(seed: int = 0, part: int = 0) -> dict:
    splits = jax.random.split(jax.random.key(seed), 6)
    own_keys = jax.random.split(jax.random.fold_in(splits[5], part), 6)
    return {
        "student_factor": centred(own_keys[0], (STUDENTS, R), 0.25, 1.5, ((0, 16),), jnp.float32),
        "level_factor": centred(own_keys[1], (LEVELS, R), 0.25, 1.5, ((0, 16),), jnp.float32),
        "block_position": draw_block_position(jax.random.fold_in(jax.random.fold_in(splits[5], part), 71), part),
        "block_count": draw_block_count(jax.random.fold_in(jax.random.fold_in(splits[5], part), 71), part),
        "outcome": set_ends((jax.random.randint(own_keys[4], (N_STU, N_LVL, MAXB, BLK, BLK), 0, 2) < 1).astype(jnp.int32), jax.random.fold_in(own_keys[4], 1), 0, 1),
    }


learn_rate = 0.05
decay_rate = 0.1


def reference(student_factor, level_factor, block_position, block_count, outcome):
    tiles = N_STU * N_LVL
    across = LVL_PANEL // BLK
    flat = jnp.arange(tiles * MAXB, dtype=jnp.int32)
    tile_id = flat // MAXB
    slot_id = flat % MAXB
    position = block_position.reshape(tiles * MAXB).astype(jnp.int32)
    counted = block_count.reshape(tiles).astype(jnp.int32)
    usable = slot_id < counted[tile_id]
    row_start = ((tile_id // N_LVL) * STU_PANEL + (position // across) * BLK).astype(jnp.int32)
    col_start = ((tile_id % N_LVL) * LVL_PANEL + (position % across) * BLK).astype(jnp.int32)
    labels = outcome.reshape(tiles * MAXB, BLK, BLK)
    zero_index = jnp.zeros((), jnp.int32)

    def one_step(students, levels):
        stu_half = students.astype(jnp.bfloat16)
        lvl_half = levels.astype(jnp.bfloat16)

        def visit(carry, item):
            grad_stu, grad_lvl = carry
            first_row, first_col, usable_now, label = item
            stu_block = lax.dynamic_slice(stu_half, (first_row, zero_index), (BLK, R))
            lvl_block = lax.dynamic_slice(lvl_half, (first_col, zero_index), (BLK, R))
            logit = jnp.dot(stu_block, lvl_block.T, preferred_element_type=jnp.float32)
            residual = jnp.where(usable_now, jax.nn.sigmoid(logit) - label.astype(jnp.float32), 0.0 * logit).astype(jnp.bfloat16)
            part_stu = jnp.dot(residual, lvl_block, preferred_element_type=jnp.float32)
            part_lvl = jnp.dot(residual.T, stu_block, preferred_element_type=jnp.float32)
            old_stu = lax.dynamic_slice(grad_stu, (first_row, zero_index), (BLK, R))
            old_lvl = lax.dynamic_slice(grad_lvl, (first_col, zero_index), (BLK, R))
            grad_stu = lax.dynamic_update_slice(grad_stu, old_stu + part_stu, (first_row, zero_index))
            grad_lvl = lax.dynamic_update_slice(grad_lvl, old_lvl + part_lvl, (first_col, zero_index))
            return (grad_stu, grad_lvl), None

        start = (jnp.zeros(students.shape, jnp.float32), jnp.zeros(levels.shape, jnp.float32))
        (grad_stu, grad_lvl), _ = lax.scan(visit, start, (row_start, col_start, usable, labels))
        students = students - learn_rate * (grad_stu + decay_rate * students)
        levels = levels - learn_rate * (grad_lvl + decay_rate * levels)
        return students, levels

    students, levels = student_factor, level_factor
    for step in range(ITERS):
        students, levels = one_step(students, levels)
    return students, levels
```

```python
import functools

import jax
import jax.numpy as jnp
from jax import lax
from jax.experimental import pallas as pl
from jax.experimental.pallas import tpu as pltpu
from jax.sharding import PartitionSpec as P

ITERS = 2
GROUP = 4

learn_rate = 0.05
decay_rate = 0.1

F32, BF16 = jnp.float32, jnp.bfloat16
NN = (((1,), (0,)), ((), ()))
NT = (((1,), (1,)), ((), ()))
TN = (((0,), (0,)), ((), ()))


def dot(a, b, dims):
    return lax.dot_general(a, b, dims, preferred_element_type=F32)


def vmem():
    return pl.BlockSpec(memory_space=pltpu.VMEM)


def smem():
    return pl.BlockSpec(memory_space=pltpu.SMEM)


def call(body, out_shape, scalars, arrays, scratch=()):
    many = isinstance(out_shape, tuple)
    return pl.pallas_call(
        body,
        out_shape=out_shape,
        in_specs=[smem()] * len(scalars) + [vmem()] * len(arrays),
        out_specs=(vmem(),) * len(out_shape) if many else vmem(),
        scratch_shapes=list(scratch),
        compiler_params=pltpu.CompilerParams(vmem_limit_bytes=48 * 2**20),
    )(*scalars, *arrays)


def sds(shape, dtype):
    return jax.ShapeDtypeStruct(tuple(shape), dtype)


def cast_body(x, y):
    y[...] = x[...].astype(y.dtype)


def sign_body(outcome, sign):
    sign[...] = (1 - 2 * outcome[...]).astype(F32).astype(BF16)


def swap(x, axis, n, k):
    return lax.ppermute(x, axis, [(i, i ^ k) for i in range(n)])


def residual_body(n_lvl, n_stu, blk, position, count, sign, *refs):
    stu_parts, refs = refs[:n_lvl], refs[n_lvl:]
    lvl_parts, refs = refs[:n_stu], refs[n_stu:]
    res, grad, stu, lvl, acc = refs
    me_l, me_s = lax.axis_index("lvl"), lax.axis_index("stu")
    own = stu_parts[0].shape[0]
    for k, part in enumerate(stu_parts):
        stu[pl.ds(pl.multiple_of((me_l ^ k) * own, own), own), :] = part[...]
    half = lvl_parts[0].shape[0]
    for k, part in enumerate(lvl_parts):
        lvl[pl.ds(pl.multiple_of((me_s ^ k) * half, half), half), :] = part[...]
    acc[...] = jnp.zeros_like(acc)
    across = lvl.shape[0] // blk
    used = count[0]

    def step(i, _):
        got = []
        for g in range(GROUP):
            b = i * GROUP + g
            p = position[b]
            row = pl.multiple_of((p // across) * blk, blk)
            col = pl.multiple_of((p % across) * blk, blk)
            u, v = stu[pl.ds(row, blk), :], lvl[pl.ds(col, blk), :]
            two = jnp.tanh(0.5 * dot(u, v, NT)) + sign[b].astype(F32)
            two = jnp.where(b < used, two, 0.0).astype(BF16)
            res[b] = two
            got.append((row, dot(two, v, NN)))
        for row, part in got:
            acc[pl.ds(row, blk), :] += part
        return 0

    lax.fori_loop(0, (used + GROUP - 1) // GROUP, step, 0)
    grad[...] = acc[...].astype(BF16).reshape(grad.shape)


def level_body(blk, position, count, res, stu, keep, send, acc):
    me_s = lax.axis_index("stu")
    acc[...] = jnp.zeros_like(acc)
    across = acc.shape[0] // blk
    used = count[0]

    def step(i, _):
        got = []
        for g in range(GROUP):
            b = i * GROUP + g
            p = position[b]
            row = pl.multiple_of((p // across) * blk, blk)
            col = pl.multiple_of((p % across) * blk, blk)
            got.append((col, dot(res[b], stu[pl.ds(row, blk), :], TN)))
        for col, part in got:
            acc[pl.ds(col, blk), :] += part
        return 0

    lax.fori_loop(0, (used + GROUP - 1) // GROUP, step, 0)
    half = keep.shape[0]
    keep[...] = acc[pl.ds(pl.multiple_of(me_s * half, half), half), :]
    send[...] = acc[pl.ds(pl.multiple_of((me_s ^ 1) * half, half), half), :].astype(BF16)


def after(own, grad_twice):
    return own - learn_rate * (0.5 * grad_twice + decay_rate * own)


def settle_student_body(own, got, new, low):
    grad = got[0].astype(F32)
    for k in range(1, got.shape[0]):
        grad += got[k].astype(F32)
    value = after(own[...], grad)
    new[...] = value
    low[...] = value.astype(BF16)


def settle_level_body(own, keep, got, new, low):
    value = after(own[...], keep[...] + got[...].astype(F32))
    new[...] = value
    low[...] = value.astype(BF16)


def per_device(n_lvl, n_stu, student_factor, level_factor, block_position, block_count, outcome):
    blk = outcome.shape[-1]
    slots = outcome.shape[2]
    stu_own, lvl_own = student_factor, level_factor
    rank = stu_own.shape[1]
    position, count = block_position.reshape(-1), block_count.reshape(-1)
    stu_rows, lvl_rows = n_lvl * stu_own.shape[0], n_stu * lvl_own.shape[0]
    stu_low = call(cast_body, sds(stu_own.shape, BF16), (), (stu_own,))
    lvl_low = call(cast_body, sds(lvl_own.shape, BF16), (), (lvl_own,))
    sign = call(
        sign_body, sds((slots, blk, blk), BF16), (), (outcome.reshape(slots, blk, blk),)
    )
    for step in range(ITERS):
        lvl_parts = [lvl_low] + [swap(lvl_low, "stu", n_stu, k) for k in range(1, n_stu)]
        stu_parts = [stu_low] + [swap(stu_low, "lvl", n_lvl, k) for k in range(1, n_lvl)]
        res, grad, stu_panel = call(
            functools.partial(residual_body, n_lvl, n_stu, blk),
            (
                sds((slots, blk, blk), BF16),
                sds((n_lvl,) + stu_own.shape, BF16),
                sds((stu_rows, rank), BF16),
            ),
            (position, count),
            (sign, *stu_parts, *lvl_parts),
            (pltpu.VMEM((lvl_rows, rank), BF16), pltpu.VMEM((stu_rows, rank), F32)),
        )
        got = lax.all_to_all(grad, "lvl", 0, 0)
        keep, send = call(
            functools.partial(level_body, blk),
            (sds(lvl_own.shape, F32), sds(lvl_own.shape, BF16)),
            (position, count),
            (res, stu_panel),
            (pltpu.VMEM((lvl_rows, rank), F32),),
        )
        came = swap(send, "stu", n_stu, 1)
        lvl_own, lvl_low = call(
            settle_level_body,
            (sds(lvl_own.shape, F32), sds(lvl_own.shape, BF16)),
            (),
            (lvl_own, keep, came),
        )
        stu_own, stu_low = call(
            settle_student_body,
            (sds(stu_own.shape, F32), sds(stu_own.shape, BF16)),
            (),
            (stu_own, got),
        )
    return (stu_own, lvl_own)


def solution(mesh):
    return jax.shard_map(
        functools.partial(per_device, mesh.shape["lvl"], mesh.shape["stu"]),
        mesh=mesh,
        in_specs=(
            P(("groups", "stu", "lvl"), None),
            P(("groups", "lvl", "stu"), None),
            P(("groups", "stu"), "lvl", None),
            P(("groups", "stu"), "lvl"),
            P(("groups", "stu"), "lvl", None, None, None),
        ),
        out_specs=(P(("groups", "stu", "lvl"), None), P(("groups", "lvl", "stu"), None)),
        check_vma=False,
    )
```

```python
import functools
import math

import jax
import jax.numpy as jnp
from jax import lax
from jax.experimental import pallas as pl
from jax.experimental.pallas import tpu as pltpu
from jax.sharding import PartitionSpec as P

ITERS = 2

learn_rate = 0.05
decay_rate = 0.1

F32, BF16 = jnp.float32, jnp.bfloat16
NN = (((1,), (0,)), ((), ()))
NT = (((1,), (1,)), ((), ()))
TN = (((0,), (0,)), ((), ()))


def dot(a, b, dims):
    return lax.dot_general(a, b, dims, preferred_element_type=F32)


def vmem():
    return pl.BlockSpec(memory_space=pltpu.VMEM)


def smem():
    return pl.BlockSpec(memory_space=pltpu.SMEM)


def sds(shape, dtype):
    return jax.ShapeDtypeStruct(tuple(shape), dtype)


def call(body, out_shape, scalars, arrays, scratch=(), cost=10000000000):
    room = sum(
        math.prod(x.shape) * jnp.dtype(x.dtype).itemsize for x in (*out_shape, *arrays, *scratch)
    )
    return pl.pallas_call(
        body,
        out_shape=tuple(out_shape),
        in_specs=[smem()] * len(scalars) + [vmem()] * len(arrays),
        out_specs=(vmem(),) * len(out_shape),
        scratch_shapes=list(scratch),
        cost_estimate=pl.CostEstimate(flops=cost, bytes_accessed=0, transcendentals=0),
        compiler_params=pltpu.CompilerParams(vmem_limit_bytes=room + 4 * 2**20),
    )(*scalars, *arrays)


def swap(x, axis, n, k):
    return lax.ppermute(x, axis, [(i, i ^ k) for i in range(n)])


def window(ref, place, size):
    return ref[pl.ds(pl.multiple_of(place * size, size), size), :]


def cast_body(stu, lvl, stu_low, lvl_low):
    stu_low[...] = stu[...].astype(BF16)
    lvl_low[...] = lvl[...].astype(BF16)


def sign_body(position, count, outcome, sign):
    sign[...] = jnp.zeros_like(sign)

    def step(b, _):
        sign[position[b]] = (1 - 2 * outcome[b]).astype(F32).astype(BF16)
        return 0

    lax.fori_loop(0, count[0], step, 0)


def panel_body(mine, other, panel):
    half, me = mine.shape[0], lax.axis_index("stu")
    panel[pl.ds(pl.multiple_of(me * half, half), half), :] = mine[...]
    panel[pl.ds(pl.multiple_of((me ^ 1) * half, half), half), :] = other[...]


def rows_body(odd, blk, n, *refs):
    parts, (lvl, sign), refs = refs[:n], refs[n : n + 2], refs[n + 2 :]
    res, stu, grads = refs
    own = parts[0].shape[0]
    owned, across = own // blk, lvl.shape[0] // blk
    wide = 2 if across % 2 == 0 else 1
    me = lax.axis_index("lvl")
    for i in range(n):
        stu[i * own : (i + 1) * own, :] = parts[i][...]
    for i in range(n):
        for q in range(owned):
            at = i * own + q * blk
            u = stu[at : at + blk, :]
            first = ((me ^ (2 * i + odd)) * owned + q) * across
            total = None
            for c in range(0, across, wide):
                v = lvl[c * blk : (c + wide) * blk, :]
                t = jnp.tanh(0.5 * dot(u, v, NT))
                twos = []
                for w in range(wide):
                    s = sign[first + c + w].astype(F32)
                    two = jnp.where(s == 0, 0.0, t[:, w * blk : (w + 1) * blk] + s).astype(BF16)
                    res[at : at + blk, (c + w) * blk : (c + w + 1) * blk] = two
                    twos.append(two)
                part = dot(jnp.concatenate(twos, 1), v, NN)
                total = part if total is None else total + part
            rows = slice(q * blk, (q + 1) * blk)
            grads[i, rows, :] = total.astype(grads.dtype)


def add_body(mine, other, *sums):
    for i, total in enumerate(sums):
        total[...] = (mine[i] + other[i].astype(F32)).astype(total.dtype)


def level_body(res0, stu0, res1, stu1, keep, send, acc):
    me, half = lax.axis_index("stu"), keep.shape[0]
    width = acc.shape[0] // 4

    def step(i, _):
        at = pl.ds(pl.multiple_of(i * width, width), width)
        acc[at, :] = dot(res0[:, at], stu0[...], TN) + dot(res1[:, at], stu1[...], TN)
        return 0

    lax.fori_loop(0, 4, step, 0)
    keep[...] = window(acc, me, half)
    send[...] = window(acc, me ^ 1, half).astype(BF16)


def settle_body(n_out, own, *refs):
    got, outs = refs[:-n_out], refs[-n_out:]
    grad = got[0][...].astype(F32)
    for other in got[1:]:
        grad += other[...].astype(F32)
    value = own[...] - learn_rate * (0.5 * grad + decay_rate * own[...])
    for out in outs:
        out[...] = value.astype(out.dtype)


def per_device(n_lvl, n_stu, order, student_factor, level_factor, block_position, block_count, outcome):
    blk, slots = outcome.shape[-1], outcome.shape[2]
    stu_own, lvl_own = student_factor, level_factor
    own, rank = stu_own.shape
    half = lvl_own.shape[0]
    lvl_rows = n_stu * half
    blocks = n_lvl * own // blk * (lvl_rows // blk)
    stu_low, lvl_low = call(
        cast_body, (sds((own, rank), BF16), sds((half, rank), BF16)), (), (stu_own, lvl_own)
    )
    (sign,) = call(
        sign_body,
        [sds((blocks, blk, blk), BF16)],
        (block_position.reshape(-1), block_count.reshape(-1)),
        (outcome.reshape(slots, blk, blk),),
    )
    for step in range(ITERS):
        last = step == ITERS - 1
        kinds = (F32,) if last else (F32, BF16)
        came = {k: swap(stu_low, "lvl", n_lvl, k) for k in order}
        came[0] = stu_low
        (panel,) = call(
            panel_body,
            [sds((lvl_rows, rank), BF16)],
            (),
            (lvl_low, swap(lvl_low, "stu", n_stu, 1)),
        )
        n = n_lvl // 2
        shapes = (sds((n * own, lvl_rows), BF16), sds((n * own, rank), BF16))
        res1, stu1, grad = call(
            functools.partial(rows_body, 1, blk, n),
            (*shapes, sds((n, own, rank), BF16)),
            (),
            (*(came[k] for k in range(1, n_lvl, 2)), panel, sign),
        )
        added = swap(grad, "lvl", n_lvl, 1)
        res0, stu0, grad = call(
            functools.partial(rows_body, 0, blk, n),
            (*shapes, sds((n, own, rank), F32)),
            (),
            (*(came[k] for k in range(0, n_lvl, 2)), panel, sign),
        )
        grads = call(
            add_body,
            (sds((own, rank), F32), *[sds((own, rank), BF16)] * (n - 1)),
            (),
            (grad, added),
        )
        back = [grads[0]] + [swap(grads[i], "lvl", n_lvl, 2 * i) for i in range(1, n)]
        keep, send = call(
            level_body,
            (sds((half, rank), F32), sds((half, rank), BF16)),
            (),
            (res0, stu0, res1, stu1),
            (pltpu.VMEM((lvl_rows, rank), F32),),
        )
        lvl_own, *lows = call(
            functools.partial(settle_body, len(kinds)),
            [sds((half, rank), kind) for kind in kinds],
            (),
            (lvl_own, keep, swap(send, "stu", n_stu, 1)),
        )
        lvl_low = lows[0] if lows else None
        stu_own, *lows = call(
            functools.partial(settle_body, len(kinds)),
            [sds((own, rank), kind) for kind in kinds],
            (),
            (stu_own, *back),
        )
        stu_low = lows[0] if lows else None
    return (stu_own, lvl_own)


def solution(mesh):
    n_lvl, n_stu = mesh.shape["lvl"], mesh.shape["stu"]
    order = sorted(range(1, n_lvl), reverse=True)
    return jax.shard_map(
        functools.partial(per_device, n_lvl, n_stu, order),
        mesh=mesh,
        in_specs=(
            P(("groups", "stu", "lvl"), None),
            P(("groups", "lvl", "stu"), None),
            P(("groups", "stu"), "lvl", None),
            P(("groups", "stu"), "lvl"),
            P(("groups", "stu"), "lvl", None, None, None),
        ),
        out_specs=(P(("groups", "stu", "lvl"), None), P(("groups", "lvl", "stu"), None)),
        check_vma=False,
    )
```

```python
import functools
import math

import jax
import jax.numpy as jnp
from jax import lax
from jax.experimental import pallas as pl
from jax.experimental.pallas import tpu as pltpu
from jax.sharding import PartitionSpec as P

ITERS = 2
COST = 10**10

learn_rate = 0.05
decay_rate = 0.1

F32, BF16 = jnp.float32, jnp.bfloat16
NN = (((1,), (0,)), ((), ()))
NT = (((1,), (1,)), ((), ()))
TN = (((0,), (0,)), ((), ()))


def dot(a, b, dims):
    return lax.dot_general(a, b, dims, preferred_element_type=F32)


def vmem():
    return pl.BlockSpec(memory_space=pltpu.VMEM)


def smem():
    return pl.BlockSpec(memory_space=pltpu.SMEM)


def sds(shape, dtype):
    return jax.ShapeDtypeStruct(tuple(shape), dtype)


def call(body, out_shape, scalars, arrays, scratch=()):
    room = sum(
        math.prod(x.shape) * jnp.dtype(x.dtype).itemsize for x in (*out_shape, *arrays, *scratch)
    )
    return pl.pallas_call(
        body,
        out_shape=tuple(out_shape),
        in_specs=[smem()] * len(scalars) + [vmem()] * len(arrays),
        out_specs=(vmem(),) * len(out_shape),
        scratch_shapes=list(scratch),
        cost_estimate=pl.CostEstimate(flops=COST, bytes_accessed=0, transcendentals=0),
        compiler_params=pltpu.CompilerParams(vmem_limit_bytes=room + 4 * 2**20),
    )(*scalars, *arrays)


def swap(x, axis, n, k):
    return lax.ppermute(x, axis, [(i, i ^ k) for i in range(n)])


def window(ref, place, size):
    return ref[pl.ds(pl.multiple_of(place * size, size), size), :]


def cast_body(rows, low):
    low[...] = rows[...].astype(BF16)


def sign_body(position, count, outcome, sign):
    sign[...] = jnp.zeros_like(sign)

    def step(b, _):
        sign[position[b]] = (1 - 2 * outcome[b]).astype(F32).astype(BF16)
        return 0

    lax.fori_loop(0, count[0], step, 0)


def panel_body(mine, other, panel):
    half, me = mine.shape[0], lax.axis_index("stu")
    panel[pl.ds(pl.multiple_of(me * half, half), half), :] = mine[...]
    panel[pl.ds(pl.multiple_of((me ^ 1) * half, half), half), :] = other[...]


def turned(n):
    return [*range(n // 2, n), *range(n // 2)]


def rows_body(partners, blk, *refs):
    n = len(partners)
    parts, (lvl, sign), refs = refs[:n], refs[n : n + 2], refs[n + 2 :]
    res, stu, grads = refs
    own = parts[0].shape[0]
    owned, across = own // blk, lvl.shape[0] // blk
    wide = 2 if across % 2 == 0 else 1
    me = lax.axis_index("lvl")
    for part, i in zip(parts, turned(n)):
        stu[i * own : (i + 1) * own, :] = part[...]
    for i in range(n):
        for q in range(owned):
            at = i * own + q * blk
            u = stu[at : at + blk, :]
            first = ((me ^ partners[i]) * owned + q) * across
            total = None
            for c in range(0, across, wide):
                v = lvl[c * blk : (c + wide) * blk, :]
                t = jnp.tanh(0.5 * dot(u, v, NT))
                twos = []
                for w in range(wide):
                    s = sign[first + c + w].astype(F32)
                    two = jnp.where(s == 0, 0.0, t[:, w * blk : (w + 1) * blk] + s).astype(BF16)
                    res[at : at + blk, (c + w) * blk : (c + w + 1) * blk] = two
                    twos.append(two)
                part = dot(jnp.concatenate(twos, 1), v, NN)
                total = part if total is None else total + part
            rows = slice(q * blk, (q + 1) * blk)
            grads[i, rows, :] = total.astype(grads.dtype)


def add_body(mine, other, *sums):
    for i, total in enumerate(sums):
        total[...] = (mine[i] + other[i].astype(F32)).astype(total.dtype)


def level_body(n, *refs):
    res, stu, (keep, send, acc) = refs[:n], refs[n : 2 * n], refs[2 * n :]
    me, half = lax.axis_index("stu"), keep.shape[0]
    width = acc.shape[0] // 4

    def step(i, _):
        at = pl.ds(pl.multiple_of(i * width, width), width)
        total = dot(res[0][:, at], stu[0][...], TN)
        for i in range(1, n):
            total += dot(res[i][:, at], stu[i][...], TN)
        acc[at, :] = total
        return 0

    lax.fori_loop(0, 4, step, 0)
    keep[...] = window(acc, me, half)
    send[...] = window(acc, me ^ 1, half).astype(BF16)


def settle_body(n_out, own, *refs):
    got, outs = refs[:-n_out], refs[-n_out:]
    grad = got[0][...].astype(F32)
    for other in got[1:]:
        grad += other[...].astype(F32)
    value = own[...] - learn_rate * (0.5 * grad + decay_rate * own[...])
    for out in outs:
        out[...] = value.astype(out.dtype)


def per_device(n_lvl, n_stu, groups, student_factor, level_factor, block_position, block_count, outcome):
    blk, slots = outcome.shape[-1], outcome.shape[2]
    stu_own, lvl_own = student_factor, level_factor
    own, rank = stu_own.shape
    half = lvl_own.shape[0]
    lvl_rows = n_stu * half
    blocks = n_lvl * own // blk * (lvl_rows // blk)
    (stu_low,) = call(cast_body, [sds((own, rank), BF16)], (), (stu_own,))
    later, _ = lax.optimization_barrier((lvl_own, stu_low))
    (lvl_low,) = call(cast_body, [sds((half, rank), BF16)], (), (later,))
    (sign,) = call(
        sign_body,
        [sds((blocks, blk, blk), BF16)],
        (block_position.reshape(-1), block_count.reshape(-1)),
        (outcome.reshape(slots, blk, blk),),
    )
    for step in range(ITERS):
        last = step == ITERS - 1
        kinds = (F32,) if last else (F32, BF16)
        came = {k: swap(stu_low, "lvl", n_lvl, k) if k else stu_low for k in range(n_lvl)}
        (panel,) = call(
            panel_body,
            [sds((lvl_rows, rank), BF16)],
            (),
            (lvl_low, swap(lvl_low, "stu", n_stu, 1)),
        )
        back, res, stu = [], [], []
        for evens in groups:
            made = []
            for partners, kind in (([k ^ 1 for k in evens], BF16), (evens, F32)):
                rows = len(partners) * own
                *panels, grad = call(
                    functools.partial(rows_body, partners, blk),
                    (
                        sds((rows, lvl_rows), BF16),
                        sds((rows, rank), BF16),
                        sds((len(partners), own, rank), kind),
                    ),
                    (),
                    (*(came[partners[i]] for i in turned(len(partners))), panel, sign),
                )
                res.append(panels[0])
                stu.append(panels[1])
                made.append(grad)
            sums = call(
                add_body,
                [sds((own, rank), BF16 if k else F32) for k in evens],
                (),
                (made[1], swap(made[0], "lvl", n_lvl, 1)),
            )
            back += [swap(x, "lvl", n_lvl, k) if k else x for k, x in zip(evens, sums)]
        keep, send = call(
            functools.partial(level_body, len(res)),
            (sds((half, rank), F32), sds((half, rank), BF16)),
            (),
            (*res, *stu),
            (pltpu.VMEM((lvl_rows, rank), F32),),
        )
        lvl_own, *lows = call(
            functools.partial(settle_body, len(kinds)),
            [sds((half, rank), kind) for kind in kinds],
            (),
            (lvl_own, keep, swap(send, "stu", n_stu, 1)),
        )
        lvl_low = lows[0] if lows else None
        stu_own, *lows = call(
            functools.partial(settle_body, len(kinds)),
            [sds((own, rank), kind) for kind in kinds],
            (),
            (stu_own, *back),
        )
        stu_low = lows[0] if lows else None
    return (stu_own, lvl_own)


def solution(mesh):
    n_lvl, n_stu = mesh.shape["lvl"], mesh.shape["stu"]
    evens = sorted(range(0, n_lvl, 2), reverse=True)
    groups = (evens,)
    return jax.shard_map(
        functools.partial(per_device, n_lvl, n_stu, groups),
        mesh=mesh,
        in_specs=(
            P(("groups", "stu", "lvl"), None),
            P(("groups", "lvl", "stu"), None),
            P(("groups", "stu"), "lvl", None),
            P(("groups", "stu"), "lvl"),
            P(("groups", "stu"), "lvl", None, None, None),
        ),
        out_specs=(P(("groups", "stu", "lvl"), None), P(("groups", "lvl", "stu"), None)),
        check_vma=False,
    )
```

```python
import functools
import math

import jax
import jax.numpy as jnp
from jax import lax
from jax.experimental import pallas as pl
from jax.experimental.pallas import tpu as pltpu
from jax.sharding import PartitionSpec as P

ITERS = 2
TALL = 2
COST = 10**10

learn_rate = 0.05
decay_rate = 0.1

F32, BF16 = jnp.float32, jnp.bfloat16
NN = (((1,), (0,)), ((), ()))
NT = (((1,), (1,)), ((), ()))
TN = (((0,), (0,)), ((), ()))


def dot(a, b, dims):
    return lax.dot_general(a, b, dims, preferred_element_type=F32)


def vmem():
    return pl.BlockSpec(memory_space=pltpu.VMEM)


def smem():
    return pl.BlockSpec(memory_space=pltpu.SMEM)


def sds(shape, dtype):
    return jax.ShapeDtypeStruct(tuple(shape), dtype)


def call(body, out_shape, scalars, arrays, scratch=()):
    room = sum(
        math.prod(x.shape) * jnp.dtype(x.dtype).itemsize for x in (*out_shape, *arrays, *scratch)
    )
    return pl.pallas_call(
        body,
        out_shape=tuple(out_shape),
        in_specs=[smem()] * len(scalars) + [vmem()] * len(arrays),
        out_specs=(vmem(),) * len(out_shape),
        scratch_shapes=list(scratch),
        cost_estimate=pl.CostEstimate(flops=COST, bytes_accessed=0, transcendentals=0),
        compiler_params=pltpu.CompilerParams(vmem_limit_bytes=room + 4 * 2**20),
    )(*scalars, *arrays)


def swap(x, axis, n, k):
    return lax.ppermute(x, axis, [(i, i ^ k) for i in range(n)])


def window(ref, place, size):
    return ref[pl.ds(pl.multiple_of(place * size, size), size), :]


def cast_body(rows, low):
    low[...] = rows[...].astype(BF16)


def sign_body(position, count, outcome, sign):
    sign[...] = jnp.zeros_like(sign)

    def step(b, _):
        sign[position[b]] = (1 - 2 * outcome[b]).astype(F32).astype(BF16)
        return 0

    lax.fori_loop(0, count[0, 0], step, 0)


def panel_body(mine, other, panel):
    half, me = mine.shape[0], lax.axis_index("stu")
    panel[pl.ds(pl.multiple_of(me * half, half), half), :] = mine[...]
    panel[pl.ds(pl.multiple_of((me ^ 1) * half, half), half), :] = other[...]


def turned(n):
    return [*range(n // 2, n), *range(n // 2)]


def rows_body(partners, blk, *refs):
    n = len(partners)
    parts, (lvl, sign), refs = refs[:n], refs[n : n + 2], refs[n + 2 :]
    res, stu, grads = refs
    own = parts[0].shape[0]
    owned, across = own // blk, lvl.shape[0] // blk
    wide = 2 if across % 2 == 0 else 1
    me = lax.axis_index("lvl")
    for part, i in zip(parts, turned(n)):
        stu[i * own : (i + 1) * own, :] = part[...]
    rows = n * own
    tall = min(TALL * blk, rows)
    for at in range(0, rows, tall):
        u = stu[at : at + tall, :]
        total = None
        for c in range(0, across, wide):
            v = lvl[c * blk : (c + wide) * blk, :]
            t = jnp.tanh(0.5 * dot(u, v, NT))
            for g in range(0, tall, blk):
                i, q = divmod((at + g) // blk, owned)
                first = ((me ^ partners[i]) * owned + q) * across
                for w in range(wide):
                    s = sign[first + c + w].astype(F32)
                    two = jnp.where(s == 0, 0.0, t[g : g + blk, w * blk : (w + 1) * blk] + s)
                    res[at + g : at + g + blk, (c + w) * blk : (c + w + 1) * blk] = two.astype(BF16)
            part = dot(res[at : at + tall, c * blk : (c + wide) * blk], v, NN)
            total = part if total is None else total + part
        grads[at // own : (at + tall) // own] = total.astype(grads.dtype).reshape(-1, own, lvl.shape[1])


def add_body(mine, other, *sums):
    for i, total in enumerate(sums):
        total[...] = (mine[i] + other[i].astype(F32)).astype(total.dtype)


def level_body(n, *refs):
    res, stu, (keep, send, acc) = refs[:n], refs[n : 2 * n], refs[2 * n :]
    me, half = lax.axis_index("stu"), keep.shape[0]
    total = dot(res[0][...], stu[0][...], TN)
    for i in range(1, n):
        total += dot(res[i][...], stu[i][...], TN)
    acc[...] = total
    keep[...] = window(acc, me, half)
    send[...] = window(acc, me ^ 1, half).astype(BF16)


def settle_body(n_out, own, *refs):
    got, outs = refs[:-n_out], refs[-n_out:]
    grad = got[0][...].astype(F32)
    for other in got[1:]:
        grad += other[...].astype(F32)
    value = own[...] - learn_rate * (0.5 * grad + decay_rate * own[...])
    for out in outs:
        out[...] = value.astype(out.dtype)


def per_device(n_lvl, n_stu, groups, student_factor, level_factor, block_position, block_count, outcome):
    blk, slots = outcome.shape[-1], outcome.shape[2]
    stu_own, lvl_own = student_factor, level_factor
    own, rank = stu_own.shape
    half = lvl_own.shape[0]
    lvl_rows = n_stu * half
    blocks = n_lvl * own // blk * (lvl_rows // blk)
    (stu_low,) = call(cast_body, [sds((own, rank), BF16)], (), (stu_own,))
    later, _ = lax.optimization_barrier((lvl_own, stu_low))
    (lvl_low,) = call(cast_body, [sds((half, rank), BF16)], (), (later,))
    (sign,) = call(
        sign_body,
        [sds((blocks, blk, blk), BF16)],
        (block_position.reshape(-1), block_count),
        (outcome.reshape(slots, blk, blk),),
    )
    for step in range(ITERS):
        last = step == ITERS - 1
        kinds = (F32,) if last else (F32, BF16)
        came = {k: swap(stu_low, "lvl", n_lvl, k) if k else stu_low for k in range(n_lvl)}
        (panel,) = call(
            panel_body,
            [sds((lvl_rows, rank), BF16)],
            (),
            (lvl_low, swap(lvl_low, "stu", n_stu, 1)),
        )
        back, res, stu = [], [], []
        for evens in groups:
            made = []
            for partners, kind in (([k ^ 1 for k in evens], BF16), (evens, F32)):
                rows = len(partners) * own
                *panels, grad = call(
                    functools.partial(rows_body, partners, blk),
                    (
                        sds((rows, lvl_rows), BF16),
                        sds((rows, rank), BF16),
                        sds((len(partners), own, rank), kind),
                    ),
                    (),
                    (*(came[partners[i]] for i in turned(len(partners))), panel, sign),
                )
                res.append(panels[0])
                stu.append(panels[1])
                made.append(grad)
            sums = call(
                add_body,
                [sds((own, rank), BF16 if k else F32) for k in evens],
                (),
                (made[1], swap(made[0], "lvl", n_lvl, 1)),
            )
            back += [swap(x, "lvl", n_lvl, k) if k else x for k, x in zip(evens, sums)]
        keep, send = call(
            functools.partial(level_body, len(res)),
            (sds((half, rank), F32), sds((half, rank), BF16)),
            (),
            (*res, *stu),
            (pltpu.VMEM((lvl_rows, rank), F32),),
        )
        lvl_own, *lows = call(
            functools.partial(settle_body, len(kinds)),
            [sds((half, rank), kind) for kind in kinds],
            (),
            (lvl_own, keep, swap(send, "stu", n_stu, 1)),
        )
        lvl_low = lows[0] if lows else None
        stu_own, *lows = call(
            functools.partial(settle_body, len(kinds)),
            [sds((own, rank), kind) for kind in kinds],
            (),
            (stu_own, *back),
        )
        stu_low = lows[0] if lows else None
    return (stu_own, lvl_own)


def solution(mesh):
    n_lvl, n_stu = mesh.shape["lvl"], mesh.shape["stu"]
    evens = sorted(range(0, n_lvl, 2), reverse=True)
    groups = (evens,)
    return jax.shard_map(
        functools.partial(per_device, n_lvl, n_stu, groups),
        mesh=mesh,
        in_specs=(
            P(("groups", "stu", "lvl"), None),
            P(("groups", "lvl", "stu"), None),
            P(("groups", "stu"), "lvl", None),
            P(("groups", "stu"), "lvl"),
            P(("groups", "stu"), "lvl", None, None, None),
        ),
        out_specs=(P(("groups", "stu", "lvl"), None), P(("groups", "lvl", "stu"), None)),
        check_vma=False,
    )
```

```python
import functools
import math

import jax
import jax.numpy as jnp
from jax import lax
from jax.experimental import pallas as pl
from jax.experimental.pallas import tpu as pltpu
from jax.sharding import PartitionSpec as P

ITERS = 2
TALL = 2
COST = 10**10

learn_rate = 0.05
decay_rate = 0.1

F32, BF16 = jnp.float32, jnp.bfloat16
NN = (((1,), (0,)), ((), ()))
NT = (((1,), (1,)), ((), ()))
TN = (((0,), (0,)), ((), ()))


def dot(a, b, dims):
    return lax.dot_general(a, b, dims, preferred_element_type=F32)


def vmem():
    return pl.BlockSpec(memory_space=pltpu.VMEM)


def smem():
    return pl.BlockSpec(memory_space=pltpu.SMEM)


def sds(shape, dtype):
    return jax.ShapeDtypeStruct(tuple(shape), dtype)


def call(body, out_shape, scalars, arrays, scratch=()):
    room = sum(
        math.prod(x.shape) * jnp.dtype(x.dtype).itemsize for x in (*out_shape, *arrays, *scratch)
    )
    return pl.pallas_call(
        body,
        out_shape=tuple(out_shape),
        in_specs=[smem()] * len(scalars) + [vmem()] * len(arrays),
        out_specs=(vmem(),) * len(out_shape),
        scratch_shapes=list(scratch),
        cost_estimate=pl.CostEstimate(flops=COST, bytes_accessed=0, transcendentals=0),
        compiler_params=pltpu.CompilerParams(vmem_limit_bytes=room + 4 * 2**20),
    )(*scalars, *arrays)


def swap(x, axis, n, k):
    return lax.ppermute(x, axis, [(i, i ^ k) for i in range(n)])


def window(ref, place, size):
    return ref[pl.ds(pl.multiple_of(place * size, size), size), :]


def cast_body(rows, low):
    low[...] = rows[...].astype(BF16)


def sign_body(position, count, outcome, sign):
    sign[...] = jnp.zeros_like(sign)

    def step(b, _):
        sign[position[b]] = (1 - 2 * outcome[b]).astype(F32).astype(BF16)
        return 0

    lax.fori_loop(0, count[0, 0], step, 0)


def panel_body(mine, other, panel):
    half, me = mine.shape[0], lax.axis_index("stu")
    panel[pl.ds(pl.multiple_of(me * half, half), half), :] = mine[...]
    panel[pl.ds(pl.multiple_of((me ^ 1) * half, half), half), :] = other[...]


def turned(n, back=False):
    far = range(n // 2)
    return [*range(n // 2, n), *(reversed(far) if back else far)]


def rows_body(partners, blk, *refs):
    n = len(partners)
    parts, (lvl, sign), refs = refs[:n], refs[n : n + 2], refs[n + 2 :]
    res, stu, grads = refs
    own = parts[0].shape[0]
    owned, across = own // blk, lvl.shape[0] // blk
    wide = 2 if across % 2 == 0 else 1
    me = lax.axis_index("lvl")
    for part, i in zip(parts, turned(n, 0 in partners)):
        stu[i * own : (i + 1) * own, :] = part[...]
    rows = n * own
    tall = min(TALL * blk, rows)
    for at in range(0, rows, tall):
        u = stu[at : at + tall, :]
        total = None
        for c in range(0, across, wide):
            v = lvl[c * blk : (c + wide) * blk, :]
            t = jnp.tanh(0.5 * dot(u, v, NT))
            for g in range(0, tall, blk):
                i, q = divmod((at + g) // blk, owned)
                first = ((me ^ partners[i]) * owned + q) * across
                for w in range(wide):
                    s = sign[first + c + w].astype(F32)
                    two = jnp.where(s == 0, 0.0, t[g : g + blk, w * blk : (w + 1) * blk] + s)
                    res[at + g : at + g + blk, (c + w) * blk : (c + w + 1) * blk] = two.astype(BF16)
            part = dot(res[at : at + tall, c * blk : (c + wide) * blk], v, NN)
            total = part if total is None else total + part
        grads[at // own : (at + tall) // own] = total.astype(grads.dtype).reshape(-1, own, lvl.shape[1])


def add_body(mine, other, *sums):
    for i, total in enumerate(sums):
        total[...] = (mine[i] + other[i].astype(F32)).astype(total.dtype)


def level_body(n, *refs):
    res, stu, (keep, send, acc) = refs[:n], refs[n : 2 * n], refs[2 * n :]
    me, half = lax.axis_index("stu"), keep.shape[0]
    total = dot(res[0][...], stu[0][...], TN)
    for i in range(1, n):
        total += dot(res[i][...], stu[i][...], TN)
    acc[...] = total
    keep[...] = window(acc, me, half)
    send[...] = window(acc, me ^ 1, half).astype(BF16)


def settle_body(n_out, own, *refs):
    got, outs = refs[:-n_out], refs[-n_out:]
    grad = got[0][...].astype(F32)
    for other in got[1:]:
        grad += other[...].astype(F32)
    value = own[...] - learn_rate * (0.5 * grad + decay_rate * own[...])
    for out in outs:
        out[...] = value.astype(out.dtype)


def per_device(n_lvl, n_stu, groups, student_factor, level_factor, block_position, block_count, outcome):
    blk, slots = outcome.shape[-1], outcome.shape[2]
    stu_own, lvl_own = student_factor, level_factor
    own, rank = stu_own.shape
    half = lvl_own.shape[0]
    lvl_rows = n_stu * half
    blocks = n_lvl * own // blk * (lvl_rows // blk)
    (stu_low,) = call(cast_body, [sds((own, rank), BF16)], (), (stu_own,))
    later, _ = lax.optimization_barrier((lvl_own, stu_low))
    (lvl_low,) = call(cast_body, [sds((half, rank), BF16)], (), (later,))
    (sign,) = call(
        sign_body,
        [sds((blocks, blk, blk), BF16)],
        (block_position.reshape(-1), block_count),
        (outcome.reshape(slots, blk, blk),),
    )
    for step in range(ITERS):
        last = step == ITERS - 1
        kinds = (F32,) if last else (F32, BF16)
        came = {k: swap(stu_low, "lvl", n_lvl, k) if k else stu_low for k in range(n_lvl)}
        (panel,) = call(
            panel_body,
            [sds((lvl_rows, rank), BF16)],
            (),
            (lvl_low, swap(lvl_low, "stu", n_stu, 1)),
        )
        back, res, stu = [], [], []
        n = n_lvl // 2
        for evens in groups:
            made = []
            for partners, kind in (([k ^ 1 for k in evens], BF16), (evens, F32)):
                rows = len(partners) * own
                *panels, grad = call(
                    functools.partial(rows_body, partners, blk),
                    (
                        sds((rows, lvl_rows), BF16),
                        sds((rows, rank), BF16),
                        sds((len(partners), own, rank), kind),
                    ),
                    (),
                    (*(came[partners[i]] for i in turned(len(partners), kind == F32)), panel, sign),
                )
                res.append(panels[0])
                stu.append(panels[1])
                made.append(grad)
            sums = call(
                add_body,
                [sds((own, rank), BF16 if k else F32) for k in evens],
                (),
                (made[1], swap(made[0], "lvl", n_lvl, 1)),
            )
            back += [swap(x, "lvl", n_lvl, k) if k else x for k, x in zip(evens, sums)]
        keep, send = call(
            functools.partial(level_body, len(res)),
            (sds((half, rank), F32), sds((half, rank), BF16)),
            (),
            (*res, *stu),
            (pltpu.VMEM((lvl_rows, rank), F32),),
        )
        lvl_own, *lows = call(
            functools.partial(settle_body, len(kinds)),
            [sds((half, rank), kind) for kind in kinds],
            (),
            (lvl_own, keep, swap(send, "stu", n_stu, 1)),
        )
        lvl_low = lows[0] if lows else None
        stu_own, *lows = call(
            functools.partial(settle_body, len(kinds)),
            [sds((own, rank), kind) for kind in kinds],
            (),
            (stu_own, *(back[i] for i in (n - 1, *reversed(range(n // 2)), *range(n // 2, n - 1)))),
        )
        stu_low = lows[0] if lows else None
    return (stu_own, lvl_own)


def solution(mesh):
    n_lvl, n_stu = mesh.shape["lvl"], mesh.shape["stu"]
    evens = sorted(range(0, n_lvl, 2), reverse=True)
    groups = (evens,)
    return jax.shard_map(
        functools.partial(per_device, n_lvl, n_stu, groups),
        mesh=mesh,
        in_specs=(
            P(("groups", "stu", "lvl"), None),
            P(("groups", "lvl", "stu"), None),
            P(("groups", "stu"), "lvl", None),
            P(("groups", "stu"), "lvl"),
            P(("groups", "stu"), "lvl", None, None, None),
        ),
        out_specs=(P(("groups", "stu", "lvl"), None), P(("groups", "lvl", "stu"), None)),
        check_vma=False,
    )
```

```python
import functools
import math

import jax
import jax.numpy as jnp
from jax import lax
from jax.experimental import pallas as pl
from jax.experimental.pallas import tpu as pltpu
from jax.sharding import PartitionSpec as P

ITERS = 2
TALL = 2
COST = 10**10

learn_rate = 0.05
decay_rate = 0.1

F32, BF16 = jnp.float32, jnp.bfloat16
NN = (((1,), (0,)), ((), ()))
NT = (((1,), (1,)), ((), ()))
TN = (((0,), (0,)), ((), ()))


def dot(a, b, dims):
    return lax.dot_general(a, b, dims, preferred_element_type=F32)


def vmem():
    return pl.BlockSpec(memory_space=pltpu.VMEM)


def smem():
    return pl.BlockSpec(memory_space=pltpu.SMEM)


def sds(shape, dtype):
    return jax.ShapeDtypeStruct(tuple(shape), dtype)


def call(body, out_shape, scalars, arrays, scratch=(), cost=COST):
    room = sum(
        math.prod(x.shape) * jnp.dtype(x.dtype).itemsize for x in (*out_shape, *arrays, *scratch)
    )
    return pl.pallas_call(
        body,
        out_shape=tuple(out_shape),
        in_specs=[smem()] * len(scalars) + [vmem()] * len(arrays),
        out_specs=(vmem(),) * len(out_shape),
        scratch_shapes=list(scratch),
        cost_estimate=pl.CostEstimate(flops=cost, bytes_accessed=0, transcendentals=0),
        compiler_params=pltpu.CompilerParams(vmem_limit_bytes=room + 4 * 2**20),
    )(*scalars, *arrays)


def swap(x, axis, n, k):
    return lax.ppermute(x, axis, [(i, i ^ k) for i in range(n)])


def window(ref, place, size):
    return ref[pl.ds(pl.multiple_of(place * size, size), size), :]


def cast_body(scale, rows, low):
    low[...] = (scale * rows[...]).astype(BF16)


def sign_body(position, count, outcome, sign):
    sign[...] = jnp.zeros_like(sign)

    def step(b, _):
        sign[position[b]] = (1 - 2 * outcome[b]).astype(F32).astype(BF16)
        return 0

    lax.fori_loop(0, count[0, 0], step, 0)


def panel_body(mine, other, panel):
    half, me = mine.shape[0], lax.axis_index("stu")
    panel[pl.ds(pl.multiple_of(me * half, half), half), :] = mine[...]
    panel[pl.ds(pl.multiple_of((me ^ 1) * half, half), half), :] = other[...]


def turned(n, back=False):
    far = range(n // 2)
    return [*range(n // 2, n), *(reversed(far) if back else far)]


def rows_body(partners, blk, *refs):
    n = len(partners)
    parts, (lvl, sign), refs = refs[:n], refs[n : n + 2], refs[n + 2 :]
    res, stu, grads = refs
    own = parts[0].shape[0]
    owned, across = own // blk, lvl.shape[0] // blk
    wide = 2 if across % 2 == 0 else 1
    me = lax.axis_index("lvl")
    for part, i in zip(parts, turned(n, 0 in partners)):
        stu[i * own : (i + 1) * own, :] = part[...]
    rows = n * own
    tall = min(TALL * blk, rows)
    for at in range(0, rows, tall):
        u = stu[at : at + tall, :]
        total = None
        for c in range(0, across, wide):
            v = lvl[c * blk : (c + wide) * blk, :]
            t = jnp.tanh(dot(u, v, NT))
            for g in range(0, tall, blk):
                i, q = divmod((at + g) // blk, owned)
                first = ((me ^ partners[i]) * owned + q) * across
                for w in range(wide):
                    s = sign[first + c + w].astype(F32)
                    two = jnp.where(s == 0, 0.0, t[g : g + blk, w * blk : (w + 1) * blk] + s)
                    res[at + g : at + g + blk, (c + w) * blk : (c + w + 1) * blk] = two.astype(BF16)
            part = dot(res[at : at + tall, c * blk : (c + wide) * blk], v, NN)
            total = part if total is None else total + part
        grads[at // own : (at + tall) // own] = total.astype(grads.dtype).reshape(-1, own, lvl.shape[1])


def add_body(mine, other, *sums):
    for i, total in enumerate(sums):
        total[...] = (mine[i] + other[i].astype(F32)).astype(total.dtype)


def level_body(n, *refs):
    res, stu, (keep, send, acc) = refs[:n], refs[n : 2 * n], refs[2 * n :]
    me, half = lax.axis_index("stu"), keep.shape[0]
    total = dot(res[0][...], stu[0][...], TN)
    for i in range(1, n):
        total += dot(res[i][...], stu[i][...], TN)
    acc[...] = total
    keep[...] = window(acc, me, half)
    send[...] = window(acc, me ^ 1, half).astype(BF16)


def settle_body(n_out, times, scale, own, *refs):
    got, outs = refs[:-n_out], refs[-n_out:]
    grad = got[0][...].astype(F32)
    for other in got[1:]:
        grad += other[...].astype(F32)
    value = own[...] - learn_rate * (times * grad + decay_rate * own[...])
    for out in outs:
        out[...] = (value if out.dtype == F32 else scale * value).astype(out.dtype)


def per_device(n_lvl, n_stu, groups, student_factor, level_factor, block_position, block_count, outcome):
    blk, slots = outcome.shape[-1], outcome.shape[2]
    stu_own, lvl_own = student_factor, level_factor
    own, rank = stu_own.shape
    half = lvl_own.shape[0]
    lvl_rows = n_stu * half
    blocks = n_lvl * own // blk * (lvl_rows // blk)
    (stu_low,) = call(functools.partial(cast_body, 0.5), [sds((own, rank), BF16)], (), (stu_own,))
    later, _ = lax.optimization_barrier((lvl_own, stu_low))
    (lvl_low,) = call(functools.partial(cast_body, 1.0), [sds((half, rank), BF16)], (), (later,))
    (sign,) = call(
        sign_body,
        [sds((blocks, blk, blk), BF16)],
        (block_position.reshape(-1), block_count),
        (outcome.reshape(slots, blk, blk),),
    )
    for step in range(ITERS):
        last = step == ITERS - 1
        kinds = (F32,) if last else (F32, BF16)
        came = {k: swap(stu_low, "lvl", n_lvl, k) if k else stu_low for k in range(n_lvl)}
        (panel,) = call(
            panel_body,
            [sds((lvl_rows, rank), BF16)],
            (),
            (lvl_low, swap(lvl_low, "stu", n_stu, 1)),
        )
        back, res, stu = [], [], []
        n = n_lvl // 2
        for evens in groups:
            made = []
            for partners, kind in (([k ^ 1 for k in evens], BF16), (evens, F32)):
                rows = len(partners) * own
                *panels, grad = call(
                    functools.partial(rows_body, partners, blk),
                    (
                        sds((rows, lvl_rows), BF16),
                        sds((rows, rank), BF16),
                        sds((len(partners), own, rank), kind),
                    ),
                    (),
                    (*(came[partners[i]] for i in turned(len(partners), kind == F32)), panel, sign),
                )
                res.append(panels[0])
                stu.append(panels[1])
                made.append(grad)
            sums = call(
                add_body,
                [sds((own, rank), BF16 if k else F32) for k in evens],
                (),
                (made[1], swap(made[0], "lvl", n_lvl, 1)),
            )
            back += [swap(x, "lvl", n_lvl, k) if k else x for k, x in zip(evens, sums)]
        keep, send = call(
            functools.partial(level_body, len(res)),
            (sds((half, rank), F32), sds((half, rank), BF16)),
            (),
            (*res, *stu),
            (pltpu.VMEM((lvl_rows, rank), F32),),
        )
        lvl_own, *lows = call(
            functools.partial(settle_body, len(kinds), 1.0, 1.0),
            [sds((half, rank), kind) for kind in kinds],
            (),
            (lvl_own, keep, swap(send, "stu", n_stu, 1)),
        )
        lvl_low = lows[0] if lows else None
        stu_own, *lows = call(
            functools.partial(settle_body, len(kinds), 0.5, 0.5),
            [sds((own, rank), kind) for kind in kinds],
            (),
            (stu_own, *(back[i] for i in (n - 1, *reversed(range(n // 2)), *range(n // 2, n - 1)))),
            cost=8 * COST,
        )
        stu_low = lows[0] if lows else None
    return (stu_own, lvl_own)


def solution(mesh):
    n_lvl, n_stu = mesh.shape["lvl"], mesh.shape["stu"]
    evens = sorted(range(0, n_lvl, 2), reverse=True)
    groups = (evens,)
    return jax.shard_map(
        functools.partial(per_device, n_lvl, n_stu, groups),
        mesh=mesh,
        in_specs=(
            P(("groups", "stu", "lvl"), None),
            P(("groups", "lvl", "stu"), None),
            P(("groups", "stu"), "lvl", None),
            P(("groups", "stu"), "lvl"),
            P(("groups", "stu"), "lvl", None, None, None),
        ),
        out_specs=(P(("groups", "stu", "lvl"), None), P(("groups", "lvl", "stu"), None)),
        check_vma=False,
    )
```

```python
import functools
import math

import jax
import jax.numpy as jnp
from jax import lax
from jax.experimental import pallas as pl
from jax.experimental.pallas import tpu as pltpu
from jax.sharding import PartitionSpec as P

ITERS = 2
TALL = 2
COST = 3 * 10**10

learn_rate = 0.05
decay_rate = 0.1

F32, BF16 = jnp.float32, jnp.bfloat16
NN = (((1,), (0,)), ((), ()))
NT = (((1,), (1,)), ((), ()))
TN = (((0,), (0,)), ((), ()))


def dot(a, b, dims):
    return lax.dot_general(a, b, dims, preferred_element_type=F32)


def vmem():
    return pl.BlockSpec(memory_space=pltpu.VMEM)


def smem():
    return pl.BlockSpec(memory_space=pltpu.SMEM)


def sds(shape, dtype):
    return jax.ShapeDtypeStruct(tuple(shape), dtype)


def call(body, out_shape, scalars, arrays, scratch=(), cost=COST):
    room = sum(
        math.prod(x.shape) * jnp.dtype(x.dtype).itemsize for x in (*out_shape, *arrays, *scratch)
    )
    return pl.pallas_call(
        body,
        out_shape=tuple(out_shape),
        in_specs=[smem()] * len(scalars) + [vmem()] * len(arrays),
        out_specs=(vmem(),) * len(out_shape),
        scratch_shapes=list(scratch),
        cost_estimate=pl.CostEstimate(flops=cost, bytes_accessed=0, transcendentals=0),
        compiler_params=pltpu.CompilerParams(vmem_limit_bytes=room + 4 * 2**20),
    )(*scalars, *arrays)


def swap(x, axis, n, k):
    return lax.ppermute(x, axis, [(i, i ^ k) for i in range(n)])


def window(ref, place, size):
    return ref[pl.ds(pl.multiple_of(place * size, size), size), :]


def cast_body(scale, rows, low):
    low[...] = (scale * rows[...]).astype(BF16)


def sign_body(position, count, outcome, sign):
    sign[...] = jnp.zeros_like(sign)

    def step(b, _):
        sign[position[b]] = (1 - 2 * outcome[b]).astype(F32).astype(BF16)
        return 0

    lax.fori_loop(0, count[0, 0], step, 0)


def panel_body(mine, other, panel):
    half, me = mine.shape[0], lax.axis_index("stu")
    panel[pl.ds(pl.multiple_of(me * half, half), half), :] = mine[...]
    panel[pl.ds(pl.multiple_of((me ^ 1) * half, half), half), :] = other[...]


def turned(n, back=False):
    far = range(n // 2)
    return [*range(n // 2, n), *(reversed(far) if back else far)]


def rows_body(partners, blk, *refs):
    n = len(partners)
    parts, (lvl, sign), refs = refs[:n], refs[n : n + 2], refs[n + 2 :]
    res, stu, grads = refs
    own = parts[0].shape[0]
    owned, across = own // blk, lvl.shape[0] // blk
    wide = 2 if across % 2 == 0 else 1
    me = lax.axis_index("lvl")
    for part, i in zip(parts, turned(n, 0 in partners)):
        stu[i * own : (i + 1) * own, :] = part[...]
    rows = n * own
    tall = min(TALL * blk, rows)
    for at in range(0, rows, tall):
        u = stu[at : at + tall, :]
        total = None
        for c in range(0, across, wide):
            v = lvl[c * blk : (c + wide) * blk, :]
            t = jnp.tanh(dot(u, v, NT))
            for g in range(0, tall, blk):
                i, q = divmod((at + g) // blk, owned)
                first = ((me ^ partners[i]) * owned + q) * across
                for w in range(wide):
                    s = sign[first + c + w].astype(F32)
                    two = jnp.where(s == 0, 0.0, t[g : g + blk, w * blk : (w + 1) * blk] + s)
                    res[at + g : at + g + blk, (c + w) * blk : (c + w + 1) * blk] = two.astype(BF16)
            part = dot(res[at : at + tall, c * blk : (c + wide) * blk], v, NN)
            total = part if total is None else total + part
        grads[at // own : (at + tall) // own] = total.astype(grads.dtype).reshape(-1, own, lvl.shape[1])


def add_body(mine, other, *sums):
    for i, total in enumerate(sums):
        total[...] = (mine[i] + other[i].astype(F32)).astype(total.dtype)


def level_body(n, *refs):
    res, stu, (keep, send, acc) = refs[:n], refs[n : 2 * n], refs[2 * n :]
    me, half = lax.axis_index("stu"), keep.shape[0]
    total = dot(res[0][...], stu[0][...], TN)
    for i in range(1, n):
        total += dot(res[i][...], stu[i][...], TN)
    acc[...] = total
    keep[...] = window(acc, me, half)
    send[...] = window(acc, me ^ 1, half).astype(BF16)


def settle_body(n_out, times, scale, own, *refs):
    got, outs = refs[:-n_out], refs[-n_out:]
    grad = got[0][...].astype(F32)
    for other in got[1:]:
        grad += other[...].astype(F32)
    value = own[...] - learn_rate * (times * grad + decay_rate * own[...])
    for out in outs:
        out[...] = (value if out.dtype == F32 else scale * value).astype(out.dtype)


def per_device(n_lvl, n_stu, groups, student_factor, level_factor, block_position, block_count, outcome):
    blk, slots = outcome.shape[-1], outcome.shape[2]
    stu_own, lvl_own = student_factor, level_factor
    own, rank = stu_own.shape
    half = lvl_own.shape[0]
    lvl_rows = n_stu * half
    blocks = n_lvl * own // blk * (lvl_rows // blk)
    (stu_low,) = call(functools.partial(cast_body, 0.5), [sds((own, rank), BF16)], (), (stu_own,))
    later, _ = lax.optimization_barrier((lvl_own, stu_low))
    (lvl_low,) = call(functools.partial(cast_body, 1.0), [sds((half, rank), BF16)], (), (later,))
    (sign,) = call(
        sign_body,
        [sds((blocks, blk, blk), BF16)],
        (block_position.reshape(-1), block_count),
        (outcome.reshape(slots, blk, blk),),
    )
    for step in range(ITERS):
        last = step == ITERS - 1
        kinds = (F32,) if last else (F32, BF16)
        came = {k: swap(stu_low, "lvl", n_lvl, k) if k else stu_low for k in range(n_lvl)}
        (panel,) = call(
            panel_body,
            [sds((lvl_rows, rank), BF16)],
            (),
            (lvl_low, swap(lvl_low, "stu", n_stu, 1)),
        )
        back, res, stu = [], [], []
        n = n_lvl // 2
        for evens in groups:
            made = []
            for partners, kind in (([k ^ 1 for k in evens], BF16), (evens, F32)):
                rows = len(partners) * own
                *panels, grad = call(
                    functools.partial(rows_body, partners, blk),
                    (
                        sds((rows, lvl_rows), BF16),
                        sds((rows, rank), BF16),
                        sds((len(partners), own, rank), kind),
                    ),
                    (),
                    (*(came[partners[i]] for i in turned(len(partners), kind == F32)), panel, sign),
                )
                res.append(panels[0])
                stu.append(panels[1])
                made.append(grad)
            sums = call(
                add_body,
                [sds((own, rank), BF16 if k else F32) for k in evens],
                (),
                (made[1], swap(made[0], "lvl", n_lvl, 1)),
            )
            back += [swap(x, "lvl", n_lvl, k) if k else x for k, x in zip(evens, sums)]
        keep, send = call(
            functools.partial(level_body, len(res)),
            (sds((half, rank), F32), sds((half, rank), BF16)),
            (),
            (*res, *stu),
            (pltpu.VMEM((lvl_rows, rank), F32),),
        )
        lvl_own, *lows = call(
            functools.partial(settle_body, len(kinds), 1.0, 1.0),
            [sds((half, rank), kind) for kind in kinds],
            (),
            (lvl_own, keep, swap(send, "stu", n_stu, 1)),
        )
        lvl_low = lows[0] if lows else None
        stu_own, *lows = call(
            functools.partial(settle_body, len(kinds), 0.5, 0.5),
            [sds((own, rank), kind) for kind in kinds],
            (),
            (stu_own, *(back[i] for i in (n - 1, *reversed(range(n // 2)), *range(n // 2, n - 1)))),
            cost=8 * COST,
        )
        stu_low = lows[0] if lows else None
    return (stu_own, lvl_own)


def solution(mesh):
    n_lvl, n_stu = mesh.shape["lvl"], mesh.shape["stu"]
    evens = sorted(range(0, n_lvl, 2), reverse=True)
    groups = (evens,)
    return jax.shard_map(
        functools.partial(per_device, n_lvl, n_stu, groups),
        mesh=mesh,
        in_specs=(
            P(("groups", "stu", "lvl"), None),
            P(("groups", "lvl", "stu"), None),
            P(("groups", "stu"), "lvl", None),
            P(("groups", "stu"), "lvl"),
            P(("groups", "stu"), "lvl", None, None, None),
        ),
        out_specs=(P(("groups", "stu", "lvl"), None), P(("groups", "lvl", "stu"), None)),
        check_vma=False,
    )
```
